32 devices in a mesh: chan: 4 (over z), inp: 8 (over y, x, core).
Axes of the slice: x: 2, y: 2, z: 4, core: 2. Of those that a mesh axis runs over, the one named last changes fastest.
Arguments:
- voltages: int32 [2, 256, 16, 4096], P(None, 'chan', None, 'inp'), may hold values from -128 to 127
- fir_taps: float32 [4, 16], replicated, may hold values from -3 to 3
Outputs:
- visibilities: float32 [16, 2, 4096, 4096], P('chan', None, 'inp')
The draws below stay inside these ranges and needn't reach their ends.
All inputs are finite; a program needn't handle non-finite values.
Results may differ from the reference program's by a relative error of at most 0.0036.
Values may be sent and summed in bfloat16 or wider, within the bound.
No kernel may reach another device: no remote copies, remote signals or barrier semaphores. Data moves between devices by JAX's collectives and lax.ppermute only.
A program may use at most 256 MiB of HBM per device.

```python
import math
import jax
import jax.numpy as jnp
from jax import lax

INPUTS = 4096
CH = 16
TAPS = 4
SPECTRA = 256


def plant(array, own_key, smallest, high):
    longest = array.shape.index(max(array.shape))
    spots = []
    for shift in (0, 1):
        where = [jax.random.randint(jax.random.fold_in(own_key, axis), (), 0, length) for axis, length in enumerate(array.shape)]
        where[longest] = (where[longest] + shift) % array.shape[longest]
        spots.append(tuple(where))
    return array.at[spots[0]].set(smallest).at[spots[1]].set(high)


def noise(stream_key, extent, deviation, limit, kind=jnp.bfloat16):
    return jnp.clip(deviation * jax.random.normal(stream_key, extent, jnp.float32), -limit, limit).astype(kind)


def setup_inputs(seed: int = 0) -> dict:
    key_list = jax.random.split(jax.random.key(seed), 3)
    voltages = plant(jax.random.randint(key_list[0], (2, SPECTRA, CH, INPUTS), -128, 128), jax.random.fold_in(key_list[0], 1), -128, 127).astype(jnp.int32)
    fir_taps = noise(key_list[1], (TAPS, CH), 0.5, 3.0, jnp.float32)
    return dict(voltages=voltages, fir_taps=fir_taps)


volt_scale = 1.0 / 256.0


def dft_tables(count):
    index = jnp.arange(count, dtype=jnp.int32)
    phase = (index[:, None] * index[None, :]) % count
    angle = phase.astype(jnp.float32) * (2.0 * math.pi / count)
    return jnp.cos(angle), jnp.sin(angle)


def transform(filtered, count):
    cosine, sine = dft_tables(count)
    real_in = filtered[0]
    imag_in = filtered[1]
    high = lax.Precision.HIGHEST
    real_out = jnp.einsum("cn,snb->csb", cosine, real_in, precision=high) + jnp.einsum("cn,snb->csb", sine, imag_in, precision=high)
    imag_out = jnp.einsum("cn,snb->csb", cosine, imag_in, precision=high) - jnp.einsum("cn,snb->csb", sine, real_in, precision=high)
    return (jnp.stack([real_out, imag_out], 1) * volt_scale).astype(jnp.bfloat16)


def reference(voltages, fir_taps):
    volts = voltages.astype(jnp.float32)
    padded = jnp.concatenate([jnp.zeros((2, TAPS - 1, CH, INPUTS), jnp.float32), volts], 1)
    filtered = fir_taps[0][None, None, :, None] * padded[:, TAPS - 1:TAPS - 1 + SPECTRA]
    for tap_index in range(1, TAPS):
        begin = TAPS - 1 - tap_index
        filtered = filtered + fir_taps[tap_index][None, None, :, None] * padded[:, begin:begin + SPECTRA]
    channelized = transform(filtered, CH)
    norm_factor = 1.0 / SPECTRA

    def one_channel(panel):
        values = panel.astype(jnp.float32)
        rotated = jnp.stack([-values[1], values[0]], 0)
        real_part = jnp.einsum("psi,psj->ij", values, values)
        imag_part = jnp.einsum("psi,psj->ij", values, rotated)
        return jnp.stack([real_part, imag_part], 0) * norm_factor

    return lax.map(one_channel, channelized)
```

```python
import functools
import math

import jax
import jax.numpy as jnp
import numpy as np
from jax import lax
from jax.experimental import pallas as pl
from jax.experimental.pallas import tpu as pltpu
from jax.sharding import PartitionSpec as P

VOLT_SCALE = 1.0 / 256.0
GROUP = 16
MIB = 1 << 20
ANY = pl.BlockSpec(memory_space=pl.ANY)


def struct(shape, dtype=jnp.bfloat16):
    return jax.ShapeDtypeStruct(shape, dtype)


def transform_rows(chans, span):
    index = np.arange(chans)
    angle = (index[:, None] * index[None, :] % chans) * (2.0 * math.pi / chans)
    cosine, sine = np.cos(angle), np.sin(angle)
    rows = np.stack([np.stack([cosine, sine], 1), np.stack([-sine, cosine], 1)], 1) * VOLT_SCALE
    rows = np.broadcast_to(rows[:, :, :, None], (chans, 2, 2, span, chans))
    return np.tile(rows.reshape(chans, 2, -1), (2, 1, 1)).astype(np.float32)


def channelize_step(shape, volts, rim, table, taps, *rest):
    devices, mine, tap_count = shape
    outs, (coarse, fine, held) = rest[:-3], rest[-3:]
    _, group, chans, width = volts.shape
    ahead = (tap_count - 1) * chans
    span = ahead + group * chans

    @pl.when(pl.program_id(0) == 0)
    def _():
        column = lax.broadcasted_iota(jnp.int32, (group, 2 * span), 1)
        column = jnp.where(column >= span, column - span, column) // chans
        row = lax.broadcasted_iota(jnp.int32, (group, 2 * span), 0)
        band = jnp.zeros((group, 2 * span), jnp.float32)
        for k in range(tap_count):
            band = band + jnp.where(column == row + (tap_count - 1 - k), taps[k : k + 1, :], 0.0)
        for c in range(table.shape[0]):
            for p in range(2):
                weights = table[c, p : p + 1, :] * band
                high = weights.astype(jnp.bfloat16)
                at = (2 * c + p) * group
                coarse[at : at + group, :] = high
                fine[at : at + group, :] = (weights - high.astype(jnp.float32)).astype(jnp.bfloat16)
        for q in range(2):
            held[q * span : q * span + ahead, :] = rim[q].reshape(ahead, width)

    @pl.when(pl.program_id(0) > 0)
    def _():
        for q in range(2):
            held[q * span : q * span + ahead, :] = held[(q + 1) * span - ahead : (q + 1) * span, :]

    for q in range(2):
        held[q * span + ahead : (q + 1) * span, :] = (
            volts[q].astype(jnp.float32).astype(jnp.bfloat16).reshape(group * chans, width)
        )
    frames = held[...]
    result = jnp.dot(coarse[...], frames, preferred_element_type=jnp.float32)
    result = result + jnp.dot(fine[...], frames, preferred_element_type=jnp.float32)
    result = result.astype(jnp.bfloat16).reshape(devices, mine, 2, group, width)
    outs[0][...] = result[0]
    for d in range(1, devices):
        for k in range(mine):
            outs[1 + (d - 1) * mine + k][...] = result[d, k]


def channelize(voltages, rim, table, taps, devices):
    _, frames, chans, width = voltages.shape
    tap_count = taps.shape[0]
    mine = chans // devices
    span = (GROUP + tap_count - 1) * chans
    flops = 2 * 2 * frames * (chans * 2) * (2 * span) * width
    outs = pl.pallas_call(
        functools.partial(channelize_step, (devices, mine, tap_count)),
        grid=(frames // GROUP,),
        in_specs=[
            pl.BlockSpec((2, GROUP, chans, width), lambda g: (0, g, 0, 0)),
            pl.BlockSpec(rim.shape, lambda g: (0, 0, 0, 0)),
            pl.BlockSpec(table.shape, lambda g: (0, 0, 0)),
            pl.BlockSpec(taps.shape, lambda g: (0, 0)),
        ],
        out_specs=[pl.BlockSpec((mine, 2, GROUP, width), lambda g: (0, 0, g, 0))]
        + [pl.BlockSpec((2, GROUP, width), lambda g: (0, g, 0))] * ((devices - 1) * mine),
        out_shape=[struct((mine, 2, frames, width))] + [struct((2, frames, width))] * ((devices - 1) * mine),
        scratch_shapes=[
            pltpu.VMEM((chans * 2 * GROUP, 2 * span), jnp.bfloat16),
            pltpu.VMEM((chans * 2 * GROUP, 2 * span), jnp.bfloat16),
            pltpu.VMEM((2 * span, width), jnp.bfloat16),
        ],
        compiler_params=pltpu.CompilerParams(vmem_limit_bytes=32 * MIB),
        cost_estimate=pl.CostEstimate(flops=flops, bytes_accessed=6 * voltages.size, transcendentals=0),
        name="channelize",
    )(voltages, rim, table, taps)
    return outs[0], [[outs[1 + (d - 1) * mine + k] for d in range(1, devices)] for k in range(mine)]


def pack_step(*refs):
    for d, ref in enumerate(refs[:-1]):
        refs[-1][d] = ref[...]


def pack(pieces):
    return pl.pallas_call(
        pack_step,
        out_shape=struct((len(pieces),) + pieces[0].shape),
        cost_estimate=pl.CostEstimate(flops=0, bytes_accessed=4 * pieces[0].size * len(pieces), transcendentals=0),
        name="pack",
    )(*pieces)


def products(left, panel, scale, out):
    rows = out.shape[2]
    result = jnp.dot(left, panel, preferred_element_type=jnp.float32) * scale
    out[0, 0] = result[:rows]
    out[0, 1] = result[rows:]


def correlate_here_step(count, scale, has_out, columns, *refs):
    near, far = refs[:count], refs[count : 2 * count]
    out, packed, left = refs[2 * count + has_out :]
    devices, _, frames, width = packed.shape[1:]
    depth = devices * 2 * frames
    for j in range(count):

        @pl.when(pl.program_id(0) == j)
        def _():
            panel = jnp.concatenate([near[j][0].reshape(2 * frames, width), far[j][...].reshape(depth - 2 * frames, width)], 0)
            packed[0] = panel.reshape(devices, 2, frames, width)
            if j == 0:
                for d in range(devices):
                    at = d * 2 * frames
                    real = panel[at : at + frames].T
                    imag = panel[at + frames : at + 2 * frames].T
                    left[:width, at : at + 2 * frames] = jnp.concatenate([real, imag], 1)
                    left[width:, at : at + 2 * frames] = jnp.concatenate([imag, -real], 1)
            products(left[...], panel, scale, out)


def correlate_there_step(scale, columns, panels, left, _, out):
    depth = left.shape[1]
    products(left[...], panels[0].reshape(depth, panels.shape[-1]), scale, out)


def correlate_here(channel, near, far, columns, out, whole):
    count = len(near)
    mine, _, frames, width = near[0].shape
    devices = far[0].shape[0] + 1
    depth = devices * 2 * frames
    has_out = out is not None
    own = lambda j, cols: (0, 0, 0, 0)
    flops = 2 * count * depth * 2 * width * width
    traffic = count * (8 * width * width + 4 * depth * width)
    return pl.pallas_call(
        functools.partial(correlate_here_step, count, 1.0 / (devices * frames), has_out),
        grid_spec=pltpu.PrefetchScalarGridSpec(
            num_scalar_prefetch=1,
            grid=(count,),
            in_specs=[pl.BlockSpec((1, 2, frames, width), lambda j, cols: (channel, 0, 0, 0))] * count
            + [pl.BlockSpec(far[0].shape, own)] * count
            + [ANY] * has_out,
            out_specs=[
                pl.BlockSpec((1, 2, width, width), lambda j, cols: (channel, 0, 0, cols[j])),
                pl.BlockSpec((1, devices, 2, frames, width), lambda j, cols: (j, 0, 0, 0, 0)),
                pl.BlockSpec((2 * width, depth), lambda j, cols: (0, 0)),
            ],
        ),
        out_shape=[whole, struct((count, devices, 2, frames, width)), struct((2 * width, depth))],
        input_output_aliases={1 + 2 * count: 0} if has_out else {},
        compiler_params=pltpu.CompilerParams(vmem_limit_bytes=40 * MIB),
        cost_estimate=pl.CostEstimate(flops=flops, bytes_accessed=traffic, transcendentals=0),
        name="correlate_here",
    )(columns, *near, *far, *([out] if has_out else []))


def correlate_there(channel, panels, left, columns, out):
    count, devices, _, frames, width = panels.shape
    depth = devices * 2 * frames
    flops = 2 * count * depth * 2 * width * width
    traffic = count * (8 * width * width + 2 * depth * width)
    return pl.pallas_call(
        functools.partial(correlate_there_step, 1.0 / (devices * frames)),
        grid_spec=pltpu.PrefetchScalarGridSpec(
            num_scalar_prefetch=1,
            grid=(count,),
            in_specs=[
                pl.BlockSpec((1, devices, 2, frames, width), lambda j, cols: (j, 0, 0, 0, 0)),
                pl.BlockSpec(left.shape, lambda j, cols: (0, 0)),
                ANY,
            ],
            out_specs=pl.BlockSpec((1, 2, width, width), lambda j, cols: (channel, 0, 0, cols[j])),
        ),
        out_shape=struct(out.shape, out.dtype),
        input_output_aliases={3: 0},
        compiler_params=pltpu.CompilerParams(vmem_limit_bytes=24 * MIB),
        cost_estimate=pl.CostEstimate(flops=flops, bytes_accessed=traffic, transcendentals=0),
        name="correlate_there",
    )(columns, panels, left, out)


def step_bits(count, core):
    bits = [1 << b for b in range(1, count.bit_length() - 1)]
    return bits if core else bits[::-1]


def source_masks(count, core):
    masks = [0]
    for bit in step_bits(count, core):
        masks += [m ^ bit for m in masks]
    return masks


def gathered(block, count):
    blocks = [block]
    orders = [step_bits(count, core) for core in (0, 1)]
    for step in range(len(orders[0])):
        pairs = [(i, i ^ orders[i % 2][step]) for i in range(count)]
        blocks += [lax.ppermute(b, "inp", pairs) for b in blocks]
    return blocks


def body(voltages, fir_taps):
    _, frames, chans, width = voltages.shape
    tap_count = fir_taps.shape[0]
    devices, count = lax.axis_size("chan"), lax.axis_size("inp")
    mine = chans // devices
    plane, place = lax.axis_index("chan"), lax.axis_index("inp")

    rim = voltages[:, frames - (tap_count - 1) :].astype(jnp.bfloat16)
    rim = lax.ppermute(rim, "chan", [(i, i + 1) for i in range(devices - 1)])
    table = transform_rows(chans, GROUP + tap_count - 1)
    table = lax.dynamic_slice_in_dim(jnp.asarray(table), plane * mine, chans, 0)
    taps = jnp.tile(fir_taps, (1, 2 * (GROUP + tap_count - 1)))
    sources = np.array(
        [
            [[i ^ m for m in source_masks(count, i % 2)], [i ^ 1 ^ m for m in source_masks(count, 1 - i % 2)]]
            for i in range(count)
        ],
        np.int32,
    )
    sources = lax.dynamic_index_in_dim(jnp.asarray(sources), place, 0, keepdims=False)

    near, turning = channelize(voltages, rim, table, taps, devices)
    nears = gathered(near, count)
    whole = struct((mine, 2, width, width * count), jnp.float32)
    other_core = [(i, i ^ 1) for i in range(count)]
    out = None
    waiting = []
    for k in range(mine):
        turned = [
            lax.ppermute(turning[k][d - 1], "chan", [(i, (i + d) % devices) for i in range(devices)])
            for d in range(1, devices)
        ]
        fars = gathered(pack(turned), count)
        out, packed, left = correlate_here(k, nears, fars, sources[0], out, whole)
        waiting.append((k, lax.ppermute(packed, "inp", other_core), left))
        if k:
            then, panels, left = waiting.pop(0)
            out = correlate_there(then, panels, left, sources[1], out)
    for then, panels, left in waiting:
        out = correlate_there(then, panels, left, sources[1], out)
    return out


def solution(mesh):
    placed = (P(None, "chan", None, "inp"), P())
    return jax.shard_map(body, mesh=mesh, in_specs=placed, out_specs=P("chan", None, "inp", None), check_vma=False)
```

```python
import functools
import math

import jax
import jax.numpy as jnp
import numpy as np
from jax import lax
from jax.experimental import pallas as pl
from jax.experimental.pallas import tpu as pltpu
from jax.sharding import PartitionSpec as P

VOLT_SCALE = 1.0 / 256.0
GROUP = 16
MIB = 1 << 20
CORRELATE_VMEM = 16 * MIB
ANY = pl.BlockSpec(memory_space=pl.ANY)
HBM = pl.BlockSpec(memory_space=pltpu.HBM)
TOKEN = jax.ShapeDtypeStruct((8, 128), jnp.float32)


def struct(shape, dtype=jnp.bfloat16):
    return jax.ShapeDtypeStruct(shape, dtype)


def transform_rows(chans, span):
    index = np.arange(chans)
    angle = (index[:, None] * index[None, :] % chans) * (2.0 * math.pi / chans)
    cosine, sine = np.cos(angle), np.sin(angle)
    rows = np.stack([np.stack([cosine, sine], 1), np.stack([-sine, cosine], 1)], 1) * VOLT_SCALE
    rows = np.broadcast_to(rows[:, :, :, None], (chans, 2, 2, span, chans))
    return np.tile(rows.reshape(chans, 2, -1), (2, 1, 1)).astype(np.float32)


def channelize_group(volts, held, weights, outs, layout):
    group, chans, width = volts.shape[1:]
    span = held.shape[0] // 2
    ahead = span - group * chans
    for q in range(2):
        held[q * span + ahead : (q + 1) * span, :] = (
            volts[q].astype(jnp.float32).astype(jnp.bfloat16).reshape(group * chans, width)
        )
    frames = held[...]
    result = jnp.dot(weights[0], frames, preferred_element_type=jnp.float32)
    result = result + jnp.dot(weights[1], frames, preferred_element_type=jnp.float32)
    devices = max(d for d, _ in layout) + 1
    result = result.astype(jnp.bfloat16).reshape(devices, -1, 2, group, width)
    for (d, channels), out in zip(layout, outs, strict=True):
        out[...] = result[d, channels[0] : channels[-1] + 1]


def channelize_inner(layout, tap_count, voltages, table, taps, *rest):
    outs, (weights, held, volts, last, sems) = rest[:-5], rest[-5:]
    slots, _, group, chans, width = volts.shape
    ahead = (tap_count - 1) * chans
    span = ahead + group * chans
    g = pl.program_id(0)

    def arrival(g):
        return pltpu.make_async_copy(voltages.at[:, pl.ds((g + 1) * group, group)], volts.at[g], sems.at[g])

    @pl.when(g == 0)
    def _():
        early = pltpu.make_async_copy(voltages.at[:, pl.ds(group - (tap_count - 1), tap_count - 1)], last, sems.at[slots])
        early.start()
        for slot in range(slots):
            arrival(slot).start()
        column = lax.broadcasted_iota(jnp.int32, (group, 2 * span), 1)
        column = jnp.where(column >= span, column - span, column) // chans
        row = lax.broadcasted_iota(jnp.int32, (group, 2 * span), 0)
        band = jnp.zeros((group, 2 * span), jnp.float32)
        for k in range(tap_count):
            band = band + jnp.where(column == row + (tap_count - 1 - k), taps[k : k + 1, :], 0.0)
        for c in range(table.shape[0]):
            for p in range(2):
                exact = table[c, p : p + 1, :] * band
                high = exact.astype(jnp.bfloat16)
                at = (2 * c + p) * group
                weights[0, at : at + group, :] = high
                weights[1, at : at + group, :] = (exact - high.astype(jnp.float32)).astype(jnp.bfloat16)
        early.wait()
        for q in range(2):
            frames = last[q].astype(jnp.float32).astype(jnp.bfloat16)
            held[q * span : q * span + ahead, :] = frames.reshape(ahead, width)

    @pl.when(g > 0)
    def _():
        for q in range(2):
            held[q * span : q * span + ahead, :] = held[(q + 1) * span - ahead : (q + 1) * span, :]

    arrival(g).wait()
    channelize_group(volts.at[g], held, weights, outs, layout)


def channelize_first(layout, voltages, rim, weights, *rest):
    outs, (held, volts, sem) = rest[len(layout) : -3], rest[-3:]
    span = held.shape[0] // 2
    ahead = span - volts.shape[1] * volts.shape[2]
    arrival = pltpu.make_async_copy(voltages.at[:, pl.ds(0, volts.shape[1])], volts, sem)
    arrival.start()
    for q in range(2):
        held[q * span : q * span + ahead, :] = rim[q].reshape(ahead, rim.shape[-1])
    arrival.wait()
    channelize_group(volts, held, weights, outs, layout)


def channelize(voltages, rim, table, taps, layout):
    _, frames, chans, width = voltages.shape
    tap_count = taps.shape[0]
    span = (GROUP + tap_count - 1) * chans
    groups = frames // GROUP
    shapes = [struct((len(channels), 2, frames, width)) for _, channels in layout]
    blocks = [(len(channels), 2, GROUP, width) for _, channels in layout]
    weight_shape = (2, chans * 2 * GROUP, 2 * span)
    cost = 2 * 2 * GROUP * (chans * 2) * (2 * span) * width
    held = pltpu.VMEM((2 * span, width), jnp.bfloat16)
    block = (2, GROUP, chans, width)
    params = pltpu.CompilerParams(vmem_limit_bytes=32 * MIB)
    *outs, weights = pl.pallas_call(
        functools.partial(channelize_inner, layout, tap_count),
        grid=(groups - 1,),
        in_specs=[
            HBM,
            pl.BlockSpec(table.shape, lambda g: (0, 0, 0)),
            pl.BlockSpec(taps.shape, lambda g: (0, 0)),
        ],
        out_specs=[pl.BlockSpec(b, lambda g: (0, 0, g + 1, 0)) for b in blocks]
        + [pl.BlockSpec(weight_shape, lambda g: (0, 0, 0))],
        out_shape=shapes + [struct(weight_shape)],
        scratch_shapes=[
            held,
            pltpu.VMEM((groups - 1,) + block, jnp.int32),
            pltpu.VMEM((2, tap_count - 1, chans, width), jnp.int32),
            pltpu.SemaphoreType.DMA((groups,)),
        ],
        compiler_params=params,
        cost_estimate=pl.CostEstimate(
            flops=cost * (groups - 1), bytes_accessed=6 * voltages.size, transcendentals=0
        ),
        name="channelize_inner",
    )(voltages, table, taps)
    return pl.pallas_call(
        functools.partial(channelize_first, layout),
        grid=(1,),
        in_specs=[
            HBM,
            pl.BlockSpec(rim.shape, lambda g: (0, 0, 0, 0)),
            pl.BlockSpec(weight_shape, lambda g: (0, 0, 0)),
        ]
        + [ANY] * len(layout),
        out_specs=[pl.BlockSpec(b, lambda g: (0, 0, 0, 0)) for b in blocks],
        out_shape=shapes,
        input_output_aliases={3 + i: i for i in range(len(layout))},
        scratch_shapes=[held, pltpu.VMEM(block, jnp.int32), pltpu.SemaphoreType.DMA],
        compiler_params=params,
        cost_estimate=pl.CostEstimate(flops=cost, bytes_accessed=6 * voltages.size // groups, transcendentals=0),
        name="channelize_first",
    )(voltages, rim, weights, *outs)


def correlate_step(shape, where, token, *refs):
    works, frames, has_out, scale = shape
    refs = list(refs)
    take = lambda number: [refs.pop(0) for _ in range(number)]
    operands = {(w, job): (take(2), take(2)) for w, (_, jobs, _) in enumerate(works) for job in jobs}
    stored = [take(1)[0] if has_left else None for _, _, has_left in works]
    take(has_out)
    out, _ = take(2)
    made = [None if has_left else take(1)[0] for _, _, has_left in works]
    panel, left, results, sems, left_sems, out_sems = refs
    slots, depth, width = panel.shape
    rows = 2 * frames
    units = [(w, job, c, half) for w, (channels, jobs, _) in enumerate(works) for job in jobs for c in range(len(channels)) for half in (0, 1)]

    def arrivals(u):
        w, job, c, half = units[u]
        at = 0
        for ref in operands[w, job][half]:
            first = works[w][0][0] if ref.shape[1] > len(works[w][0]) else 0
            for d in range(ref.shape[0]):
                yield pltpu.make_async_copy(
                    ref.at[d, first + c], panel.at[u % slots, pl.ds(at * rows, rows)], sems.at[u % slots, at]
                )
                at += 1

    def departures(u):
        w, job, c, half = units[u]
        columns = pl.ds(pl.multiple_of(where[job, half] * width, width), width)
        for p in range(2):
            slot = (2 * u + p) % results.shape[0]
            yield pltpu.make_async_copy(results.at[slot], out.at[works[w][0][0] + c, p, :, columns], out_sems.at[slot])

    def stored_rows(w, c):
        return pltpu.make_async_copy(stored[w].at[c], left.at[w, c], left_sems.at[w, c])

    def made_rows(w, c):
        return pltpu.make_async_copy(left.at[w, c], made[w].at[c], left_sems.at[w, c])

    seen = set()
    behind = results.shape[0] // 2
    for u in range(min(slots, len(units))):
        w, _, c, _ = units[u]
        if stored[w] is not None and (w, c) not in seen:
            stored_rows(w, c).start()
            seen.add((w, c))
        for copy in arrivals(u):
            copy.start()
    ready = set()
    for u, (w, job, c, half) in enumerate(units):
        for copy in arrivals(u):
            copy.wait()
        if (w, c) not in ready:
            ready.add((w, c))
            if stored[w] is not None:
                stored_rows(w, c).wait()
            else:
                for at in range(0, depth, rows):
                    real = panel[u % slots, at : at + frames].T
                    imag = panel[u % slots, at + frames : at + rows].T
                    left[w, c, :width, at : at + rows] = jnp.concatenate([real, imag], 1)
                    left[w, c, width:, at : at + rows] = jnp.concatenate([imag, -real], 1)
                made_rows(w, c).start()
        if u >= behind:
            for copy in departures(u - behind):
                copy.wait()
        for p, copy in enumerate(departures(u)):
            lines = left[w, c, p * width : (p + 1) * width]
            result = jnp.dot(lines, panel[u % slots], preferred_element_type=jnp.float32) * scale
            results[(2 * u + p) % results.shape[0]] = result
            copy.start()
        later = u + slots
        if later < len(units):
            w, _, c, _ = units[later]
            if stored[w] is not None and (w, c) not in seen:
                stored_rows(w, c).start()
                seen.add((w, c))
            for copy in arrivals(later):
                copy.start()
    for u in range(max(0, len(units) - behind), len(units)):
        for copy in departures(u):
            copy.wait()
    for w, (channels, _, has_left) in enumerate(works):
        if not has_left:
            for c in range(len(channels)):
                made_rows(w, c).wait()


def correlate(works, where, token, out, whole):
    frames, width = next(iter(works[0][2].values()))[0][0].shape[-2:]
    operands = [
        p.reshape(-1, p.shape[-4], 2 * frames, width) for _, _, jobs in works for job in jobs.values() for half in job for p in half
    ]
    depth = 2 * frames * (operands[0].shape[0] + operands[1].shape[0])
    lefts = [left for _, left, _ in works if left is not None]
    has_out = out is not None
    channels = max(len(channels) for channels, _, _ in works)
    made = [struct((len(c), 2 * width, depth)) for c, left, _ in works if left is None]
    shape = ([(tuple(c), tuple(jobs), left is not None) for c, left, jobs in works], frames, has_out, 2.0 / depth)
    slots, results = 4, 4
    out, token, *made = pl.pallas_call(
        functools.partial(correlate_step, shape),
        in_specs=[pl.BlockSpec(memory_space=pltpu.SMEM), ANY] + [HBM] * (len(operands) + len(lefts) + has_out),
        out_specs=[HBM, ANY] + [HBM] * len(made),
        out_shape=[whole, TOKEN] + made,
        input_output_aliases={1: 1, **({2 + len(operands) + len(lefts): 0} if has_out else {})},
        scratch_shapes=[
            pltpu.VMEM((slots, depth, width), jnp.bfloat16),
            pltpu.VMEM((len(works), channels, 2 * width, depth), jnp.bfloat16),
            pltpu.VMEM((results, width, width), jnp.float32),
            pltpu.SemaphoreType.DMA((slots, depth // (2 * frames))),
            pltpu.SemaphoreType.DMA((len(works), channels)),
            pltpu.SemaphoreType.DMA((results,)),
        ],
        compiler_params=pltpu.CompilerParams(vmem_limit_bytes=CORRELATE_VMEM),
        cost_estimate=pl.CostEstimate(flops=0, bytes_accessed=0, transcendentals=0),
        name="correlate",
    )(where, token, *operands, *lefts, *([out] if has_out else []))
    made = iter(made)
    return out, token, [left if left is not None else next(made) for _, left, _ in works]


def step_bits(count, core):
    bits = [1 << b for b in range(1, count.bit_length() - 1)]
    return bits if core else bits[::-1]


def source_masks(count, core):
    masks = [0]
    for bit in step_bits(count, core):
        masks += [m ^ bit for m in masks]
    return masks


def moves(count):
    order = []
    for step in range(len(step_bits(count, 0))):
        order += [(block, step) for block in range(1 << step)]
    return order


def body(voltages, fir_taps):
    _, frames, chans, width = voltages.shape
    tap_count = fir_taps.shape[0]
    devices, count = lax.axis_size("chan"), lax.axis_size("inp")
    mine = chans // devices
    plane, place = lax.axis_index("chan"), lax.axis_index("inp")

    rim = voltages[:, frames - (tap_count - 1) :].astype(jnp.bfloat16)
    rim = lax.ppermute(rim, "chan", [(i, i + 1) for i in range(devices - 1)])
    table = transform_rows(chans, GROUP + tap_count - 1)
    table = lax.dynamic_slice_in_dim(jnp.asarray(table), plane * mine, chans, 0)
    taps = jnp.tile(fir_taps, (1, 2 * (GROUP + tap_count - 1)))
    sources = np.array([[i ^ m for m in source_masks(count, i % 2)] for i in range(count)], np.int32)
    sources = np.stack([sources, sources[np.arange(count) ^ 1]], 2)
    sources = lax.dynamic_index_in_dim(jnp.asarray(sources), place, 0, keepdims=False)

    halves = [range(mine)] if mine < 2 else [range(mine // 2), range(mine // 2, mine)]
    layout = [(0, range(mine))] + [(d, half) for half in halves for d in range(1, devices)]
    firsts = channelize(voltages, rim, table, taps, layout)

    def turned(piece, d):
        return lax.ppermute(piece, "chan", [(i, (i + d) % devices) for i in range(devices)])

    def swapped(block):
        return lax.ppermute(block, "inp", [(i, i ^ 1) for i in range(count)])

    orders = [step_bits(count, core) for core in (0, 1)]
    steps = moves(count)
    chips = len(steps) + 1
    whole = struct((mine, 2, width, width * count), jnp.float32)

    groups = range(1 + len(halves))
    turning = [firsts[1 + h * (devices - 1) :][: devices - 1] for h in range(len(halves))]
    here = [[] for _ in groups]
    there = [[] for _ in groups]
    jobs = [(h, m) for h in range(len(halves)) for m in range(chips)]
    lefts = {}
    state = {"out": None, "token": jnp.zeros(TOKEN.shape, TOKEN.dtype)}

    def gated(arrays):
        *arrays, state["token"] = lax.optimization_barrier((*arrays, state["token"]))
        return arrays

    def work():
        works = {}
        while jobs:
            h, m = jobs[0]
            held = (0, 1 + h)
            if any(len(there[g]) <= m for g in held):
                break
            jobs.pop(0)
            works.setdefault(h, {})[m] = [[side[g][m] for g in held] for side in (here, there)]
        if works:
            state["out"], state["token"], rows = correlate(
                [(halves[h], lefts.get(h), pairs) for h, pairs in works.items()], sources, state["token"], state["out"], whole
            )
            lefts.update(zip(works, rows))

    def one_round(sends, turns, swaps):
        sent = gated([here[g][source] for g, source, _ in sends] + [piece for _, piece in turns] + [here[g][m] for g, m in swaps])
        moved = [
            lax.ppermute(block, "inp", [(i, i ^ orders[i % 2][step]) for i in range(count)])
            for block, (_, _, step) in zip(sent, sends)
        ]
        arrived = [turned(block, d) for block, (d, _) in zip(sent[len(sends) :], turns)]
        for block, (g, _) in zip(sent[len(sends) + len(turns) :], swaps):
            there[g].append(swapped(block))
        work()
        moved = gated(moved + arrived)
        for block, (g, _, _) in zip(moved, sends):
            here[g].append(block)
        return moved[len(sends) :]

    here[0].append(firsts[0])
    swaps = [(0, 0)]
    for g in groups:
        rest = list(enumerate(turning[g], 1)) if g < len(halves) else []
        arrived = []
        pending = list(steps)
        rounds = []
        landed = 1
        while pending:
            now = [move for move in pending[:2] if move[0] < landed]
            pending = pending[len(now) :]
            landed += len(now)
            rounds.append(now)
        share = -(-len(rest) // len(rounds))
        for now in rounds:
            arrived += one_round([(g, source, step) for source, step in now], rest[:share], swaps)
            rest = rest[share:]
            swaps = [(g, len(here[g]) - len(now) + i) for i in range(len(now))]
        if arrived:
            here[g + 1] += gated([jnp.stack(arrived)])
            swaps.append((g + 1, 0))
    one_round([], [], swaps)
    return state["out"]


def solution(mesh):
    placed = (P(None, "chan", None, "inp"), P())
    return jax.shard_map(body, mesh=mesh, in_specs=placed, out_specs=P("chan", None, "inp", None), check_vma=False)
```

```python
import functools
import math

import jax
import jax.numpy as jnp
import numpy as np
from jax import lax
from jax.experimental import pallas as pl
from jax.experimental.pallas import tpu as pltpu
from jax.sharding import PartitionSpec as P

VOLT_SCALE = 1.0 / 256.0
GROUP = 16
MIB = 1 << 20
CHANNELIZE_VMEM = 32 * MIB
CORRELATE_VMEM = 18 * MIB
ANY = pl.BlockSpec(memory_space=pl.ANY)
HBM = pl.BlockSpec(memory_space=pltpu.HBM)
TOKEN = jax.ShapeDtypeStruct((8, 128), jnp.float32)


def struct(shape, dtype=jnp.bfloat16):
    return jax.ShapeDtypeStruct(shape, dtype)


def transform_rows(chans, span):
    index = np.arange(chans)
    angle = (index[:, None] * index[None, :] % chans) * (2.0 * math.pi / chans)
    cosine, sine = np.cos(angle), np.sin(angle)
    rows = np.stack([np.stack([cosine, sine], 1), np.stack([-sine, cosine], 1)], 1) * VOLT_SCALE
    rows = np.broadcast_to(rows[:, :, :, None], (chans, 2, 2, span, chans))
    return np.tile(rows.reshape(chans, 2, -1), (2, 1, 1)).astype(np.float32)


def channelize_group(volts, held, weights, outs, layout):
    group, chans, width = volts.shape[1:]
    span = held.shape[0] // 2
    ahead = span - group * chans
    for q in range(2):
        held[q * span + ahead : (q + 1) * span, :] = (
            volts[q].astype(jnp.float32).astype(jnp.bfloat16).reshape(group * chans, width)
        )
    frames = held[...]
    result = jnp.dot(weights[0], frames, preferred_element_type=jnp.float32)
    result = result + jnp.dot(weights[1], frames, preferred_element_type=jnp.float32)
    devices = max(d for d, _ in layout) + 1
    result = result.astype(jnp.bfloat16).reshape(devices, -1, 2, group, width)
    for (d, channels), out in zip(layout, outs, strict=True):
        out[...] = result[d, channels[0] : channels[-1] + 1]


def channelize_inner(layout, tap_count, voltages, table, taps, *rest):
    outs, (weights, held, volts, last, sems) = rest[:-5], rest[-5:]
    slots, _, group, chans, width = volts.shape
    ahead = (tap_count - 1) * chans
    span = ahead + group * chans
    g = pl.program_id(0)

    def arrival(g):
        return pltpu.make_async_copy(voltages.at[:, pl.ds((g + 1) * group, group)], volts.at[g], sems.at[g])

    @pl.when(g == 0)
    def _():
        early = pltpu.make_async_copy(voltages.at[:, pl.ds(group - (tap_count - 1), tap_count - 1)], last, sems.at[slots])
        early.start()
        for slot in range(slots):
            arrival(slot).start()
        column = lax.broadcasted_iota(jnp.int32, (group, 2 * span), 1)
        column = jnp.where(column >= span, column - span, column) // chans
        row = lax.broadcasted_iota(jnp.int32, (group, 2 * span), 0)
        sample = lax.broadcasted_iota(jnp.int32, (chans, 2 * span), 1) % chans
        spread = (sample == lax.broadcasted_iota(jnp.int32, (chans, 2 * span), 0)).astype(jnp.float32)
        spread_taps = jnp.dot(taps[...], spread, precision=lax.Precision.HIGHEST, preferred_element_type=jnp.float32)
        first = lax.axis_index("chan") * (chans // lax.axis_size("chan"))
        band = jnp.zeros((group, 2 * span), jnp.float32)
        for k in range(tap_count):
            band = band + jnp.where(column == row + (tap_count - 1 - k), spread_taps[k : k + 1, :], 0.0)
        for c in range(chans):
            for p in range(2):
                exact = table[first + c, p : p + 1, :] * band
                high = exact.astype(jnp.bfloat16)
                at = (2 * c + p) * group
                weights[0, at : at + group, :] = high
                weights[1, at : at + group, :] = (exact - high.astype(jnp.float32)).astype(jnp.bfloat16)
        early.wait()
        for q in range(2):
            frames = last[q].astype(jnp.float32).astype(jnp.bfloat16)
            held[q * span : q * span + ahead, :] = frames.reshape(ahead, width)

    @pl.when(g > 0)
    def _():
        for q in range(2):
            held[q * span : q * span + ahead, :] = held[(q + 1) * span - ahead : (q + 1) * span, :]

    arrival(g).wait()
    channelize_group(volts.at[g], held, weights, outs, layout)


def channelize_first(layout, voltages, rim, weights, *rest):
    outs, (held, volts, sem) = rest[len(layout) : -3], rest[-3:]
    span = held.shape[0] // 2
    ahead = span - volts.shape[1] * volts.shape[2]
    arrival = pltpu.make_async_copy(voltages.at[:, pl.ds(0, volts.shape[1])], volts, sem)
    arrival.start()
    for q in range(2):
        held[q * span : q * span + ahead, :] = rim[q].reshape(ahead, rim.shape[-1])
    arrival.wait()
    channelize_group(volts, held, weights, outs, layout)


def channelize(voltages, rim, table, taps, layout):
    _, frames, chans, width = voltages.shape
    tap_count = taps.shape[0]
    span = (GROUP + tap_count - 1) * chans
    groups = frames // GROUP
    shapes = [struct((len(channels), 2, frames, width)) for _, channels in layout]
    blocks = [(len(channels), 2, GROUP, width) for _, channels in layout]
    weight_shape = (2, chans * 2 * GROUP, 2 * span)
    cost = 2 * 2 * GROUP * (chans * 2) * (2 * span) * width
    held = pltpu.VMEM((2 * span, width), jnp.bfloat16)
    block = (2, GROUP, chans, width)
    params = pltpu.CompilerParams(vmem_limit_bytes=CHANNELIZE_VMEM)
    *outs, weights = pl.pallas_call(
        functools.partial(channelize_inner, layout, tap_count),
        grid=(groups - 1,),
        in_specs=[
            HBM,
            pl.BlockSpec(table.shape, lambda g: (0, 0, 0)),
            pl.BlockSpec(taps.shape, lambda g: (0, 0)),
        ],
        out_specs=[pl.BlockSpec(b, lambda g: (0, 0, g + 1, 0)) for b in blocks]
        + [pl.BlockSpec(weight_shape, lambda g: (0, 0, 0))],
        out_shape=shapes + [struct(weight_shape)],
        scratch_shapes=[
            held,
            pltpu.VMEM((groups - 1,) + block, jnp.int32),
            pltpu.VMEM((2, tap_count - 1, chans, width), jnp.int32),
            pltpu.SemaphoreType.DMA((groups,)),
        ],
        compiler_params=params,
        cost_estimate=pl.CostEstimate(
            flops=cost * (groups - 1), bytes_accessed=6 * voltages.size, transcendentals=0
        ),
        name="channelize_inner",
    )(voltages, table, taps)
    return pl.pallas_call(
        functools.partial(channelize_first, layout),
        grid=(1,),
        in_specs=[
            HBM,
            pl.BlockSpec(rim.shape, lambda g: (0, 0, 0, 0)),
            pl.BlockSpec(weight_shape, lambda g: (0, 0, 0)),
        ]
        + [ANY] * len(layout),
        out_specs=[pl.BlockSpec(b, lambda g: (0, 0, 0, 0)) for b in blocks],
        out_shape=shapes,
        input_output_aliases={3 + i: i for i in range(len(layout))},
        scratch_shapes=[held, pltpu.VMEM(block, jnp.int32), pltpu.SemaphoreType.DMA],
        compiler_params=params,
        cost_estimate=pl.CostEstimate(flops=cost, bytes_accessed=6 * voltages.size // groups, transcendentals=0),
        name="channelize_first",
    )(voltages, rim, weights, *outs)


def correlate_step(shape, where, token, *refs):
    works, frames, has_out, scale = shape
    refs = list(refs)
    take = lambda number: [refs.pop(0) for _ in range(number)]
    operands = {(w, job): (take(2), take(2)) for w, (_, jobs, _) in enumerate(works) for job in jobs}
    stored = [take(1)[0] if has_left else None for _, _, has_left in works]
    take(has_out)
    out, _ = take(2)
    made = [None if has_left else take(1)[0] for _, _, has_left in works]
    panel, left, results, sems, left_sems, out_sems = refs
    slots, distances, rows, width = panel.shape
    depth = distances * rows
    units = [(w, job, c, half) for w, (channels, jobs, _) in enumerate(works) for job in jobs for c in range(len(channels)) for half in (0, 1)]

    def arrivals(u):
        w, job, c, half = units[u]
        at = 0
        for i, ref in enumerate(operands[w, job][half]):
            first = works[w][0][0] if ref.shape[1] > len(works[w][0]) else 0
            yield pltpu.make_async_copy(
                ref.at[:, first + c], panel.at[u % slots, pl.ds(at, ref.shape[0])], sems.at[u % slots, i]
            )
            at += ref.shape[0]

    def departures(u):
        w, job, c, half = units[u]
        columns = pl.ds(pl.multiple_of(where[job, half] * width, width), width)
        for p in range(2):
            slot = (2 * u + p) % results.shape[0]
            yield pltpu.make_async_copy(results.at[slot], out.at[works[w][0][0] + c, p, :, columns], out_sems.at[slot])

    def stored_rows(w, c):
        return pltpu.make_async_copy(stored[w].at[c], left.at[w, c], left_sems.at[w, c])

    def made_rows(w, c):
        return pltpu.make_async_copy(left.at[w, c], made[w].at[c], left_sems.at[w, c])

    seen = set()
    behind = results.shape[0] // 2
    for u in range(min(slots, len(units))):
        w, _, c, _ = units[u]
        if stored[w] is not None and (w, c) not in seen:
            stored_rows(w, c).start()
            seen.add((w, c))
        for copy in arrivals(u):
            copy.start()
    ready = set()
    for u, (w, job, c, half) in enumerate(units):
        for copy in arrivals(u):
            copy.wait()
        if (w, c) not in ready:
            ready.add((w, c))
            if stored[w] is not None:
                stored_rows(w, c).wait()
            else:
                for d in range(distances):
                    at = d * rows
                    real = panel[u % slots, d, :frames].T
                    imag = panel[u % slots, d, frames:].T
                    left[w, c, :width, at : at + rows] = jnp.concatenate([real, imag], 1)
                    left[w, c, width:, at : at + rows] = jnp.concatenate([imag, -real], 1)
                made_rows(w, c).start()
        if u >= behind:
            for copy in departures(u - behind):
                copy.wait()
        for p, copy in enumerate(departures(u)):
            lines = left[w, c, p * width : (p + 1) * width]
            result = jnp.dot(lines, panel[u % slots].reshape(depth, width), preferred_element_type=jnp.float32) * scale
            results[(2 * u + p) % results.shape[0]] = result
            copy.start()
        later = u + slots
        if later < len(units):
            w, _, c, _ = units[later]
            if stored[w] is not None and (w, c) not in seen:
                stored_rows(w, c).start()
                seen.add((w, c))
            for copy in arrivals(later):
                copy.start()
    for u in range(max(0, len(units) - behind), len(units)):
        for copy in departures(u):
            copy.wait()
    for w, (channels, _, has_left) in enumerate(works):
        if not has_left:
            for c in range(len(channels)):
                made_rows(w, c).wait()


def correlate(works, where, token, out, whole):
    frames, width = next(iter(works[0][2].values()))[0][0].shape[-2:]
    operands = [
        p.reshape(-1, p.shape[-4], 2 * frames, width) for _, _, jobs in works for job in jobs.values() for half in job for p in half
    ]
    depth = 2 * frames * (operands[0].shape[0] + operands[1].shape[0])
    lefts = [left for _, left, _ in works if left is not None]
    has_out = out is not None
    channels = max(len(channels) for channels, _, _ in works)
    made = [struct((len(c), 2 * width, depth)) for c, left, _ in works if left is None]
    shape = ([(tuple(c), tuple(jobs), left is not None) for c, left, jobs in works], frames, has_out, 2.0 / depth)
    slots, results = 4, 8
    out, token, *made = pl.pallas_call(
        functools.partial(correlate_step, shape),
        in_specs=[pl.BlockSpec(memory_space=pltpu.SMEM), ANY] + [HBM] * (len(operands) + len(lefts) + has_out),
        out_specs=[HBM, ANY] + [HBM] * len(made),
        out_shape=[whole, TOKEN] + made,
        input_output_aliases={1: 1, **({2 + len(operands) + len(lefts): 0} if has_out else {})},
        scratch_shapes=[
            pltpu.VMEM((slots, depth // (2 * frames), 2 * frames, width), jnp.bfloat16),
            pltpu.VMEM((len(works), channels, 2 * width, depth), jnp.bfloat16),
            pltpu.VMEM((results, width, width), jnp.float32),
            pltpu.SemaphoreType.DMA((slots, 2)),
            pltpu.SemaphoreType.DMA((len(works), channels)),
            pltpu.SemaphoreType.DMA((results,)),
        ],
        compiler_params=pltpu.CompilerParams(vmem_limit_bytes=CORRELATE_VMEM),
        cost_estimate=pl.CostEstimate(flops=0, bytes_accessed=0, transcendentals=0),
        name="correlate",
    )(where, token, *operands, *lefts, *([out] if has_out else []))
    made = iter(made)
    return out, token, [left if left is not None else next(made) for _, left, _ in works]


def step_bits(count, core):
    bits = [1 << b for b in range(1, count.bit_length() - 1)]
    return bits if core else bits[::-1]


def source_masks(count, core):
    masks = [0]
    for bit in step_bits(count, core):
        masks += [m ^ bit for m in masks]
    return masks


def moves(count):
    order = []
    for step in range(len(step_bits(count, 0))):
        order += [(block, step) for block in range(1 << step)]
    return order


def body(voltages, fir_taps):
    _, frames, chans, width = voltages.shape
    tap_count = fir_taps.shape[0]
    devices, count = lax.axis_size("chan"), lax.axis_size("inp")
    mine = chans // devices
    place = lax.axis_index("inp")

    rim = voltages[:, frames - (tap_count - 1) :].astype(jnp.bfloat16)
    rim = lax.ppermute(rim, "chan", [(i, i + 1) for i in range(devices - 1)])
    table = transform_rows(chans, GROUP + tap_count - 1)
    sources = np.array([[i ^ m for m in source_masks(count, i % 2)] for i in range(count)], np.int32)
    sources = np.stack([sources, sources[np.arange(count) ^ 1]], 2)
    sources = lax.dynamic_index_in_dim(jnp.asarray(sources), place, 0, keepdims=False)

    halves = [range(mine)] if mine < 2 else [range(mine // 2), range(mine // 2, mine)]
    layout = [(0, range(mine))] + [(d, half) for half in halves for d in range(1, devices)]
    firsts = channelize(voltages, rim, jnp.asarray(table), fir_taps, layout)

    def turned(piece, d):
        return lax.ppermute(piece, "chan", [(i, (i + d) % devices) for i in range(devices)])

    def swapped(block):
        return lax.ppermute(block, "inp", [(i, i ^ 1) for i in range(count)])

    orders = [step_bits(count, core) for core in (0, 1)]
    steps = moves(count)
    chips = len(steps) + 1
    whole = struct((mine, 2, width, width * count), jnp.float32)

    groups = range(1 + len(halves))
    turning = [firsts[1 + h * (devices - 1) :][: devices - 1] for h in range(len(halves))]
    here = [[] for _ in groups]
    there = [[] for _ in groups]
    jobs = [(h, m) for h in range(len(halves)) for m in range(chips)]
    lefts = {}
    state = {"out": None, "token": jnp.zeros(TOKEN.shape, TOKEN.dtype)}

    def gated(arrays):
        *arrays, state["token"] = lax.optimization_barrier((*arrays, state["token"]))
        return arrays

    def work():
        works = {}
        while jobs:
            h, m = jobs[0]
            held = (0, 1 + h)
            if any(len(there[g]) <= m for g in held):
                break
            jobs.pop(0)
            works.setdefault(h, {})[m] = [[side[g][m] for g in held] for side in (here, there)]
        if works:
            state["out"], state["token"], rows = correlate(
                [(halves[h], lefts.get(h), pairs) for h, pairs in works.items()], sources, state["token"], state["out"], whole
            )
            lefts.update(zip(works, rows))

    def one_round(sends, turns, swaps):
        sent = gated([here[g][source] for g, source, _ in sends] + [piece for _, piece in turns] + [here[g][m] for g, m in swaps])
        moved = [
            lax.ppermute(block, "inp", [(i, i ^ orders[i % 2][step]) for i in range(count)])
            for block, (_, _, step) in zip(sent, sends)
        ]
        arrived = [turned(block, d) for block, (d, _) in zip(sent[len(sends) :], turns)]
        for block, (g, _) in zip(sent[len(sends) + len(turns) :], swaps):
            there[g].append(swapped(block))
        work()
        moved = gated(moved + arrived)
        for block, (g, _, _) in zip(moved, sends):
            here[g].append(block)
        return moved[len(sends) :]

    here[0].append(firsts[0])
    swaps = [(0, 0)]
    for g in groups:
        rest = list(enumerate(turning[g], 1)) if g < len(halves) else []
        arrived = []
        pending = list(steps)
        rounds = []
        landed = 1
        while pending:
            now = [move for move in pending[:2] if move[0] < landed]
            pending = pending[len(now) :]
            landed += len(now)
            rounds.append(now)
        share = -(-len(rest) // len(rounds))
        for now in rounds:
            arrived += one_round([(g, source, step) for source, step in now], rest[:share], swaps)
            rest = rest[share:]
            swaps = [(g, len(here[g]) - len(now) + i) for i in range(len(now))]
        if arrived:
            here[g + 1] += gated([jnp.stack(arrived)])
            swaps.append((g + 1, 0))
    one_round([], [], swaps)
    return state["out"]


def solution(mesh):
    placed = (P(None, "chan", None, "inp"), P())
    return jax.shard_map(body, mesh=mesh, in_specs=placed, out_specs=P("chan", None, "inp", None), check_vma=False)
```

```python
import functools
import math

import jax
import jax.numpy as jnp
import numpy as np
from jax import lax
from jax.experimental import pallas as pl
from jax.experimental.pallas import tpu as pltpu
from jax.sharding import PartitionSpec as P

VOLT_SCALE = 1.0 / 256.0
GROUP = 16
MIB = 1 << 20
CHANNELIZE_VMEM = 32 * MIB
CORRELATE_VMEM = 18 * MIB
ANY = pl.BlockSpec(memory_space=pl.ANY)
HBM = pl.BlockSpec(memory_space=pltpu.HBM)
TOKEN = jax.ShapeDtypeStruct((8, 128), jnp.float32)


def struct(shape, dtype=jnp.bfloat16):
    return jax.ShapeDtypeStruct(shape, dtype)


def channelize_group(volts, held, weights, outs, layout):
    group, chans, width = volts.shape[1:]
    span = held.shape[0] // 2
    ahead = span - group * chans
    for q in range(2):
        held[q * span + ahead : (q + 1) * span, :] = (
            volts[q].astype(jnp.float32).astype(jnp.bfloat16).reshape(group * chans, width)
        )
    frames = held[...]
    result = jnp.dot(weights[0], frames, preferred_element_type=jnp.float32)
    result = result + jnp.dot(weights[1], frames, preferred_element_type=jnp.float32)
    devices = max(d for d, _ in layout) + 1
    result = result.astype(jnp.bfloat16).reshape(devices, -1, 2, group, width)
    for (d, channels), out in zip(layout, outs, strict=True):
        out[...] = result[d, channels[0] : channels[-1] + 1]


def channelize_inner(layout, tap_count, voltages, taps, *rest):
    outs, (weights, held, volts, last, sems) = rest[:-5], rest[-5:]
    slots, _, group, chans, width = volts.shape
    ahead = (tap_count - 1) * chans
    span = ahead + group * chans
    g = pl.program_id(0)

    def arrival(g):
        return pltpu.make_async_copy(voltages.at[:, pl.ds((g + 1) * group, group)], volts.at[g], sems.at[g])

    @pl.when(g == 0)
    def _():
        early = pltpu.make_async_copy(voltages.at[:, pl.ds(group - (tap_count - 1), tap_count - 1)], last, sems.at[slots])
        early.start()
        for slot in range(slots):
            arrival(slot).start()
        column = lax.broadcasted_iota(jnp.int32, (group, 2 * span), 1)
        column = jnp.where(column >= span, column - span, column) // chans
        row = lax.broadcasted_iota(jnp.int32, (group, 2 * span), 0)
        sample = lax.broadcasted_iota(jnp.int32, (chans, 2 * span), 1) % chans
        spread = (sample == lax.broadcasted_iota(jnp.int32, (chans, 2 * span), 0)).astype(jnp.float32)
        spread_taps = jnp.dot(taps[...], spread, precision=lax.Precision.HIGHEST, preferred_element_type=jnp.float32)
        first = lax.axis_index("chan") * (chans // lax.axis_size("chan"))
        band = jnp.zeros((group, 2 * span), jnp.float32)
        for k in range(tap_count):
            band = band + jnp.where(column == row + (tap_count - 1 - k), spread_taps[k : k + 1, :], 0.0)
        row = lax.broadcasted_iota(jnp.int32, (2 * chans, 2 * span), 0)
        column = lax.broadcasted_iota(jnp.int32, (2 * chans, 2 * span), 1)
        quarters = (row % 2) - (column >= span).astype(jnp.int32)
        turn = ((first + row // 2) * (column % chans) + quarters * (chans // 4) + chans) % chans
        basis = jnp.zeros((2 * chans, 2 * span), jnp.float32)
        for m in range(chans):
            basis = jnp.where(turn == m, math.cos(2.0 * math.pi * m / chans) * VOLT_SCALE, basis)
        for c in range(chans):
            for p in range(2):
                exact = basis[2 * c + p : 2 * c + p + 1, :] * band
                high = exact.astype(jnp.bfloat16)
                at = (2 * c + p) * group
                weights[0, at : at + group, :] = high
                weights[1, at : at + group, :] = (exact - high.astype(jnp.float32)).astype(jnp.bfloat16)
        early.wait()
        for q in range(2):
            frames = last[q].astype(jnp.float32).astype(jnp.bfloat16)
            held[q * span : q * span + ahead, :] = frames.reshape(ahead, width)

    @pl.when(g > 0)
    def _():
        for q in range(2):
            held[q * span : q * span + ahead, :] = held[(q + 1) * span - ahead : (q + 1) * span, :]

    arrival(g).wait()
    channelize_group(volts.at[g], held, weights, outs, layout)


def channelize_first(layout, voltages, rim, weights, *rest):
    outs, (held, volts, sem) = rest[len(layout) : -3], rest[-3:]
    span = held.shape[0] // 2
    ahead = span - volts.shape[1] * volts.shape[2]
    arrival = pltpu.make_async_copy(voltages.at[:, pl.ds(0, volts.shape[1])], volts, sem)
    arrival.start()
    for q in range(2):
        held[q * span : q * span + ahead, :] = rim[q].reshape(ahead, rim.shape[-1])
    arrival.wait()
    channelize_group(volts, held, weights, outs, layout)


def channelize(voltages, rim, taps, layout):
    _, frames, chans, width = voltages.shape
    tap_count = taps.shape[0]
    span = (GROUP + tap_count - 1) * chans
    groups = frames // GROUP
    shapes = [struct((len(channels), 2, frames, width)) for _, channels in layout]
    blocks = [(len(channels), 2, GROUP, width) for _, channels in layout]
    weight_shape = (2, chans * 2 * GROUP, 2 * span)
    cost = 2 * 2 * GROUP * (chans * 2) * (2 * span) * width
    held = pltpu.VMEM((2 * span, width), jnp.bfloat16)
    block = (2, GROUP, chans, width)
    params = pltpu.CompilerParams(vmem_limit_bytes=CHANNELIZE_VMEM)
    *outs, weights = pl.pallas_call(
        functools.partial(channelize_inner, layout, tap_count),
        grid=(groups - 1,),
        in_specs=[
            HBM,
            pl.BlockSpec(taps.shape, lambda g: (0, 0)),
        ],
        out_specs=[pl.BlockSpec(b, lambda g: (0, 0, g + 1, 0)) for b in blocks]
        + [pl.BlockSpec(weight_shape, lambda g: (0, 0, 0))],
        out_shape=shapes + [struct(weight_shape)],
        scratch_shapes=[
            held,
            pltpu.VMEM((groups - 1,) + block, jnp.int32),
            pltpu.VMEM((2, tap_count - 1, chans, width), jnp.int32),
            pltpu.SemaphoreType.DMA((groups,)),
        ],
        compiler_params=params,
        cost_estimate=pl.CostEstimate(
            flops=cost * (groups - 1), bytes_accessed=6 * voltages.size, transcendentals=0
        ),
        name="channelize_inner",
    )(voltages, taps)
    return pl.pallas_call(
        functools.partial(channelize_first, layout),
        grid=(1,),
        in_specs=[
            HBM,
            pl.BlockSpec(rim.shape, lambda g: (0, 0, 0, 0)),
            pl.BlockSpec(weight_shape, lambda g: (0, 0, 0)),
        ]
        + [ANY] * len(layout),
        out_specs=[pl.BlockSpec(b, lambda g: (0, 0, 0, 0)) for b in blocks],
        out_shape=shapes,
        input_output_aliases={3 + i: i for i in range(len(layout))},
        scratch_shapes=[held, pltpu.VMEM(block, jnp.int32), pltpu.SemaphoreType.DMA],
        compiler_params=params,
        cost_estimate=pl.CostEstimate(flops=cost, bytes_accessed=6 * voltages.size // groups, transcendentals=0),
        name="channelize_first",
    )(voltages, rim, weights, *outs)


def correlate_step(shape, where, token, *refs):
    works, frames, has_out, scale = shape
    refs = list(refs)
    take = lambda number: [refs.pop(0) for _ in range(number)]
    operands = {(w, job): (take(2), take(2)) for w, (_, jobs, _) in enumerate(works) for job in jobs}
    stored = [take(1)[0] if has_left else None for _, _, has_left in works]
    take(has_out)
    out, _ = take(2)
    made = [None if has_left else take(1)[0] for _, _, has_left in works]
    panel, left, results, sems, left_sems, out_sems = refs
    slots, distances, rows, width = panel.shape
    depth = distances * rows
    units = [(w, job, c, half) for w, (channels, jobs, _) in enumerate(works) for job in jobs for c in range(len(channels)) for half in (0, 1)]

    def arrivals(u):
        w, job, c, half = units[u]
        at = 0
        for i, ref in enumerate(operands[w, job][half]):
            first = works[w][0][0] if ref.shape[1] > len(works[w][0]) else 0
            yield pltpu.make_async_copy(
                ref.at[:, first + c], panel.at[u % slots, pl.ds(at, ref.shape[0])], sems.at[u % slots, i]
            )
            at += ref.shape[0]

    def departures(u):
        w, job, c, half = units[u]
        columns = pl.ds(pl.multiple_of(where[job, half] * width, width), width)
        for p in range(2):
            slot = (2 * u + p) % results.shape[0]
            yield pltpu.make_async_copy(results.at[slot], out.at[works[w][0][0] + c, p, :, columns], out_sems.at[slot])

    def stored_rows(w, c):
        return pltpu.make_async_copy(stored[w].at[c], left.at[w, c], left_sems.at[w, c])

    def made_rows(w, c):
        return pltpu.make_async_copy(left.at[w, c], made[w].at[c], left_sems.at[w, c])

    seen = set()
    behind = results.shape[0] // 2
    for u in range(min(slots, len(units))):
        w, _, c, _ = units[u]
        if stored[w] is not None and (w, c) not in seen:
            stored_rows(w, c).start()
            seen.add((w, c))
        for copy in arrivals(u):
            copy.start()
    ready = set()
    for u, (w, job, c, half) in enumerate(units):
        for copy in arrivals(u):
            copy.wait()
        if (w, c) not in ready:
            ready.add((w, c))
            if stored[w] is not None:
                stored_rows(w, c).wait()
            else:
                for d in range(distances):
                    at = d * rows
                    real = panel[u % slots, d, :frames].T
                    imag = panel[u % slots, d, frames:].T
                    left[w, c, :width, at : at + rows] = jnp.concatenate([real, imag], 1)
                    left[w, c, width:, at : at + rows] = jnp.concatenate([imag, -real], 1)
                made_rows(w, c).start()
        if u >= behind:
            for copy in departures(u - behind):
                copy.wait()
        for p, copy in enumerate(departures(u)):
            lines = left[w, c, p * width : (p + 1) * width]
            result = jnp.dot(lines, panel[u % slots].reshape(depth, width), preferred_element_type=jnp.float32) * scale
            results[(2 * u + p) % results.shape[0]] = result
            copy.start()
        later = u + slots
        if later < len(units):
            w, _, c, _ = units[later]
            if stored[w] is not None and (w, c) not in seen:
                stored_rows(w, c).start()
                seen.add((w, c))
            for copy in arrivals(later):
                copy.start()
    for u in range(max(0, len(units) - behind), len(units)):
        for copy in departures(u):
            copy.wait()
    for w, (channels, _, has_left) in enumerate(works):
        if not has_left:
            for c in range(len(channels)):
                made_rows(w, c).wait()


def correlate(works, where, token, out, whole):
    frames, width = next(iter(works[0][2].values()))[0][0].shape[-2:]
    operands = [
        p.reshape(-1, p.shape[-4], 2 * frames, width) for _, _, jobs in works for job in jobs.values() for half in job for p in half
    ]
    depth = 2 * frames * (operands[0].shape[0] + operands[1].shape[0])
    lefts = [left for _, left, _ in works if left is not None]
    has_out = out is not None
    channels = max(len(channels) for channels, _, _ in works)
    made = [struct((len(c), 2 * width, depth)) for c, left, _ in works if left is None]
    shape = ([(tuple(c), tuple(jobs), left is not None) for c, left, jobs in works], frames, has_out, 2.0 / depth)
    slots, results = 4, 8
    out, token, *made = pl.pallas_call(
        functools.partial(correlate_step, shape),
        in_specs=[pl.BlockSpec(memory_space=pltpu.SMEM), ANY] + [HBM] * (len(operands) + len(lefts) + has_out),
        out_specs=[HBM, ANY] + [HBM] * len(made),
        out_shape=[whole, TOKEN] + made,
        input_output_aliases={1: 1, **({2 + len(operands) + len(lefts): 0} if has_out else {})},
        scratch_shapes=[
            pltpu.VMEM((slots, depth // (2 * frames), 2 * frames, width), jnp.bfloat16),
            pltpu.VMEM((len(works), channels, 2 * width, depth), jnp.bfloat16),
            pltpu.VMEM((results, width, width), jnp.float32),
            pltpu.SemaphoreType.DMA((slots, 2)),
            pltpu.SemaphoreType.DMA((len(works), channels)),
            pltpu.SemaphoreType.DMA((results,)),
        ],
        compiler_params=pltpu.CompilerParams(vmem_limit_bytes=CORRELATE_VMEM),
        cost_estimate=pl.CostEstimate(flops=0, bytes_accessed=0, transcendentals=0),
        name="correlate",
    )(where, token, *operands, *lefts, *([out] if has_out else []))
    made = iter(made)
    return out, token, [left if left is not None else next(made) for _, left, _ in works]


def step_bits(count, core):
    bits = [1 << b for b in range(1, count.bit_length() - 1)]
    return bits if core else bits[::-1]


def source_masks(count, core):
    masks = [0]
    for bit in step_bits(count, core):
        masks += [m ^ bit for m in masks]
    return masks


def moves(count):
    order = []
    for step in range(len(step_bits(count, 0))):
        order += [(block, step) for block in range(1 << step)]
    return order


def body(voltages, fir_taps):
    _, frames, chans, width = voltages.shape
    tap_count = fir_taps.shape[0]
    devices, count = lax.axis_size("chan"), lax.axis_size("inp")
    mine = chans // devices
    place = lax.axis_index("inp")

    rim = voltages[:, frames - (tap_count - 1) :].astype(jnp.bfloat16)
    rim = lax.ppermute(rim, "chan", [(i, i + 1) for i in range(devices - 1)])
    sources = np.array([[i ^ m for m in source_masks(count, i % 2)] for i in range(count)], np.int32)
    sources = np.stack([sources, sources[np.arange(count) ^ 1]], 2)
    sources = lax.dynamic_index_in_dim(jnp.asarray(sources), place, 0, keepdims=False)

    halves = [range(mine)] if mine < 2 else [range(mine // 2), range(mine // 2, mine)]
    layout = [(0, range(mine))] + [(d, half) for half in halves for d in range(1, devices)]
    firsts = channelize(voltages, rim, fir_taps, layout)

    def turned(piece, d):
        return lax.ppermute(piece, "chan", [(i, (i + d) % devices) for i in range(devices)])

    def swapped(block):
        return lax.ppermute(block, "inp", [(i, i ^ 1) for i in range(count)])

    orders = [step_bits(count, core) for core in (0, 1)]
    steps = moves(count)
    chips = len(steps) + 1
    whole = struct((mine, 2, width, width * count), jnp.float32)

    groups = range(1 + len(halves))
    turning = [firsts[1 + h * (devices - 1) :][: devices - 1] for h in range(len(halves))]
    here = [[] for _ in groups]
    there = [[] for _ in groups]
    jobs = [(h, m) for h in range(len(halves)) for m in range(chips)]
    lefts = {}
    state = {"out": None, "token": jnp.zeros(TOKEN.shape, TOKEN.dtype)}

    def gated(arrays):
        *arrays, state["token"] = lax.optimization_barrier((*arrays, state["token"]))
        return arrays

    def work():
        works = {}
        while jobs:
            h, m = jobs[0]
            held = (0, 1 + h)
            if any(len(there[g]) <= m for g in held):
                break
            jobs.pop(0)
            works.setdefault(h, {})[m] = [[side[g][m] for g in held] for side in (here, there)]
        if works:
            state["out"], state["token"], rows = correlate(
                [(halves[h], lefts.get(h), pairs) for h, pairs in works.items()], sources, state["token"], state["out"], whole
            )
            lefts.update(zip(works, rows))

    def one_round(sends, turns, swaps):
        sent = gated([here[g][source] for g, source, _ in sends] + [piece for _, piece in turns] + [here[g][m] for g, m in swaps])
        moved = [
            lax.ppermute(block, "inp", [(i, i ^ orders[i % 2][step]) for i in range(count)])
            for block, (_, _, step) in zip(sent, sends)
        ]
        arrived = [turned(block, d) for block, (d, _) in zip(sent[len(sends) :], turns)]
        for block, (g, _) in zip(sent[len(sends) + len(turns) :], swaps):
            there[g].append(swapped(block))
        work()
        moved = gated(moved + arrived)
        for block, (g, _, _) in zip(moved, sends):
            here[g].append(block)
        return moved[len(sends) :]

    here[0].append(firsts[0])
    swaps = [(0, 0)]
    for g in groups:
        rest = list(enumerate(turning[g], 1)) if g < len(halves) else []
        arrived = []
        pending = list(steps)
        rounds = []
        landed = 1
        while pending:
            now = [move for move in pending[:2] if move[0] < landed]
            pending = pending[len(now) :]
            landed += len(now)
            rounds.append(now)
        share = -(-len(rest) // len(rounds))
        for now in rounds:
            arrived += one_round([(g, source, step) for source, step in now], rest[:share], swaps)
            rest = rest[share:]
            swaps = [(g, len(here[g]) - len(now) + i) for i in range(len(now))]
        if arrived:
            here[g + 1] += gated([jnp.stack(arrived)])
            swaps.append((g + 1, 0))
    one_round([], [], swaps)
    return state["out"]


def solution(mesh):
    placed = (P(None, "chan", None, "inp"), P())
    return jax.shard_map(body, mesh=mesh, in_specs=placed, out_specs=P("chan", None, "inp", None), check_vma=False)
```
